256 devices in a mesh: dp: 8 (over y_lo, x), axial: 32 (over y_hi, z, core).
Axes of the slice: x: 4, y: 4 (y_hi: 2, y_lo: 2; y = y_hi * 2 + y_lo), z: 8, core: 2. Of those that a mesh axis runs over, the one named last changes fastest.
Arguments:
- pair_act: bfloat16 [2048, 256, 128], P(('dp', 'axial')), parts along dimension 0, may hold values from -6 to 6
- norm_gain: float32 [128], replicated, may hold values from 0.25 to 1.75
- norm_offset: float32 [128], replicated, may hold values from -3 to 3
- w_query: bfloat16 [128, 128], replicated, may hold values from -0.5 to 0.5
- w_key: bfloat16 [128, 128], replicated, may hold values from -0.5 to 0.5
- w_value: bfloat16 [128, 128], replicated, may hold values from -0.5 to 0.5
- w_bias: bfloat16 [128, 4], replicated, as said below
- w_gate: bfloat16 [128, 128], replicated, may hold values from -0.5 to 0.5
- gate_bias: float32 [128], replicated, may hold values from -4 to 4
- w_out: bfloat16 [128, 128], replicated, may hold values from -0.5 to 0.5
- out_bias: float32 [128], replicated, may hold values from -3 to 3
Outputs:
- pair_update: bfloat16 [2048, 256, 128], P(('dp', 'axial')), parts along dimension 0
The draws below stay inside these ranges and needn't reach their ends.
There are 8 independent parts, one for each index of `dp`. The reference program is written for one: setup_inputs(seed, part) draws one part's arguments, and reference() takes and returns one part's arrays. A program takes and returns all parts, laid end to end along the dimension named above; an argument that names none is the same for every part. Nothing has to cross between parts.
Inputs may be any that keep to these rules, and one draw needn't show every extreme that they name: `w_bias`: normal entries scaled by s / sqrt(128), with s between 1.5 and 50.
All inputs are finite; a program needn't handle non-finite values.
Results may differ from the reference program's by a relative error of at most 0.0024.
The reference program's roundings to bfloat16 on the way (of `normed`, `queries`, `bias_rows`, `weights` and `gated`) count: a program that leaves them out, or rounds other values in their place, can miss the bound.
Values may be sent and summed in bfloat16 or wider, within the bound.
A program may use at most 192 MiB of HBM per device.

```python
import jax
import jax.numpy as jnp
from jax import lax

C = 128
H = 4
DH = 32
RESIDUES = 256


def draw_w_bias(key, part):
    key = jax.random.fold_in(key, 7)
    base = jax.random.normal(key, (C, H), jnp.float32)
    factor = 1.5
    return (base * (factor / C ** 0.5)).astype(jnp.bfloat16)


def steps_of(own_key, shape, shards, low, largest):
    factor_of, own = 1.0, jax.random.fold_in(own_key, 6)
    for position, blocks in shards:
        steps = jnp.exp(jax.random.uniform(jax.random.fold_in(own, position), (blocks,), jnp.float32, low / len(shards), largest / len(shards)))
        factor_of = factor_of * jnp.repeat(steps, shape[position] // blocks).reshape([-1 if axis == position else 1 for axis in range(len(shape))])
    return factor_of


def scatter_about(own_key, dims, width, most, pieces=(), kind=jnp.bfloat16):
    entries = jax.random.normal(own_key, dims, jnp.float32) * width
    if len(pieces) > 0:
        entries = steps_of(own_key, dims, pieces, -0.22, 0.18) * entries
    return jnp.clip(entries, min=-most, max=most).astype(kind)


def setup_inputs(seed: int = 0, part: int = 0) -> dict:
    streams_of = jax.random.split(jax.random.key(seed), 12)
    own_keys = jax.random.split(jax.random.fold_in(streams_of[11], part), 12)
    pair_act = scatter_about(own_keys[0], (RESIDUES, RESIDUES, C), 1.0, 6.0, ((0, 32),))
    norm_gain = jnp.clip(1.0 + 0.15 * jax.random.normal(streams_of[1], (C,), jnp.float32), 0.25, 1.75)
    norm_offset = scatter_about(streams_of[2], (C,), 0.5, 3.0, (), jnp.float32)
    w_query = scatter_about(streams_of[3], (C, C), C ** -0.5, 0.5)
    w_key = scatter_about(streams_of[4], (C, C), C ** -0.5, 0.5)
    w_value = scatter_about(streams_of[5], (C, C), C ** -0.5, 0.5)
    w_bias = draw_w_bias(jax.random.fold_in(streams_of[11], 71), part)
    w_gate = scatter_about(streams_of[7], (C, C), C ** -0.5, 0.5)
    gate_bias = scatter_about(streams_of[8], (C,), 1.0, 4.0, (), jnp.float32)
    w_out = scatter_about(streams_of[9], (C, C), C ** -0.5, 0.5)
    out_bias = scatter_about(streams_of[10], (C,), 0.5, 3.0, (), jnp.float32)
    return {"pair_act": pair_act, "norm_gain": norm_gain, "norm_offset": norm_offset, "w_query": w_query, "w_key": w_key, "w_value": w_value, "w_bias": w_bias, "w_gate": w_gate, "gate_bias": gate_bias, "w_out": w_out, "out_bias": out_bias}


def normalize(pair_act, norm_gain, norm_offset):
    values_f = pair_act.astype(jnp.float32)
    average = lax.optimization_barrier(jnp.mean(values_f, axis=-1, keepdims=True))
    spread = lax.optimization_barrier(jnp.mean((values_f - average) ** 2, axis=-1, keepdims=True))
    scaled = (values_f - average) * lax.rsqrt(spread + 1e-05) * norm_gain + norm_offset
    return scaled.astype(jnp.bfloat16)

def project(normed, weight):
    flat = normed.reshape(-1, normed.shape[-1])
    return jnp.dot(flat, weight, preferred_element_type=jnp.float32).reshape(normed.shape[:-1] + (weight.shape[1],))

def reference(pair_act, norm_gain, norm_offset, w_query, w_key, w_value, w_bias, w_gate, gate_bias, w_out, out_bias):
    count = pair_act.shape[0]
    normed = normalize(pair_act, norm_gain, norm_offset)
    queries = (project(normed, w_query) * (1.0 / DH ** 0.5)).astype(jnp.bfloat16).reshape(count, count, H, DH)
    key_rows = project(normed, w_key).astype(jnp.bfloat16).reshape(count, count, H, DH)
    value_rows = project(normed, w_value).astype(jnp.bfloat16).reshape(count, count, H, DH)
    bias_rows = project(normed, w_bias).astype(jnp.bfloat16)
    gating = jax.nn.sigmoid(project(normed, w_gate) + gate_bias)

    def one_head(head_index):
        q_head = queries[:, :, head_index, :].astype(jnp.float32)
        k_head = key_rows[:, :, head_index, :].astype(jnp.float32)
        v_head = value_rows[:, :, head_index, :].astype(jnp.float32)
        b_head = bias_rows[:, :, head_index].astype(jnp.float32)
        scores = jnp.einsum('ijc,kjc->ijk', q_head, k_head) + jnp.transpose(b_head)[:, None, :]
        highest = lax.optimization_barrier(jnp.max(scores, axis=2, keepdims=True))
        expo = jnp.exp(scores - highest)
        running_sum = lax.optimization_barrier(jnp.sum(expo, axis=2))
        weights = lax.optimization_barrier(expo.astype(jnp.bfloat16)).astype(jnp.float32)
        summed = jnp.einsum('ijk,kjc->ijc', weights, v_head)
        return summed / running_sum[:, :, None]
    heads_out = lax.map(one_head, jnp.arange(H))
    attended = jnp.transpose(heads_out, (1, 2, 0, 3)).reshape(count, count, C)
    gated = (gating * attended).astype(jnp.bfloat16)
    return (project(gated, w_out) + out_bias).astype(jnp.bfloat16)
```

```python
import functools

import jax
import jax.numpy as jnp
from jax import lax
from jax.experimental import pallas as pl
from jax.experimental.pallas import tpu as pltpu
from jax.sharding import PartitionSpec as P

MESH = pl.DeviceIdType.MESH
NZ, NY, NCORE = 8, 2, 2
N = NZ * NY * NCORE
ROWS = 8
RES = 256
C = 128
H = 4
DH = 32
CHUNKS = 2
COLS = RES // N // CHUNKS
MSG = COLS * ROWS

OFFSETS = [(dz, dy, dc) for dz in range(NZ) for dy in range(NY) for dc in range(NCORE)][1:]

NT = (((1,), (1,)), ((), ()))


def dot_nt(a, b):
    return lax.dot_general(a, b, NT, preferred_element_type=jnp.float32)


def dot_nn(a, b):
    return jnp.dot(a, b, preferred_element_type=jnp.float32)


def kernel(
    x_hbm, gain_hbm, offset_hbm, wq_hbm, wk_hbm, wv_hbm, wb_hbm, wg_hbm, gb_hbm, wo_hbm, ob_hbm,
    out_ref,
    x_v, gain_v, offset_v, wq_v, wk_v, wv_v, wb_v, wg_v, gb_v, wo_v, ob_v,
    send1, recv1, send2, bias_all, bias_f, w_t, gate_bias_t,
    load_sem, s1_sem, r1_sem, s2_sem, r2_sem, bs_sem, br_sem,
):
    me = lax.axis_index("axial")
    my_y, my_z, my_c = me // (NZ * NCORE), (me // NCORE) % NZ, me % NCORE

    def other(dz, dy, dc):
        return ((my_y + dy) % NY) * (NZ * NCORE) + ((my_z + dz) % NZ) * NCORE + (my_c + dc) % NCORE

    loads = []
    for n, (src, dst) in enumerate(
        [
            (x_hbm, x_v), (gain_hbm, gain_v), (offset_hbm, offset_v), (wb_hbm, wb_v), (wq_hbm, wq_v), (wk_hbm, wk_v),
            (wv_hbm, wv_v), (wg_hbm, wg_v), (gb_hbm, gb_v), (wo_hbm, wo_v), (ob_hbm, ob_v),
        ]
    ):
        copy = pltpu.make_async_copy(src, dst, load_sem.at[n])
        copy.start()
        loads.append(copy)

    barrier = pltpu.get_barrier_semaphore()
    for off in OFFSETS:
        pl.semaphore_signal(barrier, inc=1, device_id={"axial": other(*off)}, device_id_type=MESH)

    for n in range(4):
        loads[n].wait()

    gain = gain_v[...][None]
    shift = offset_v[...][None]
    wb = wb_v[...].astype(jnp.float32)
    wb_rep = jnp.broadcast_to(wb[:, None, :], (H, ROWS, C)).reshape(H * ROWS, C)
    row_of = lax.broadcasted_iota(jnp.int32, (H * ROWS, C), 0) % ROWS
    wb_row = [jnp.where(row_of == r, wb_rep, 0.0).astype(jnp.bfloat16) for r in range(ROWS)]

    STEP = 32
    for block in range(RES // STEP):
        values = x_v[:, pl.ds(block * STEP, STEP), :].astype(jnp.float32)
        average = jnp.mean(values, axis=-1, keepdims=True)
        centred = values - average
        spread = jnp.mean(centred * centred, axis=-1, keepdims=True)
        scaled = centred * lax.rsqrt(spread + 1e-05) * gain + shift
        turned = jnp.swapaxes(scaled, 0, 1).reshape(STEP // 2, 2 * ROWS, C)
        turned = turned.astype(jnp.bfloat16).reshape(STEP * ROWS // MSG, MSG, C)
        first = block * STEP * ROWS // MSG
        send1[pl.ds(first, STEP * ROWS // MSG)] = turned
        x_v[:, pl.ds(block * STEP, STEP), :] = scaled.astype(jnp.bfloat16)

    acc = dot_nt(wb_row[0], x_v[0])
    for r in range(1, ROWS):
        acc = acc + dot_nt(wb_row[r], x_v[r])
    bias_all[my_y, my_z, my_c] = acc.astype(jnp.bfloat16)

    pl.semaphore_wait(barrier, N - 1)

    bias_sends = []

    def bias_send(src, k, n, off):
        copy = pltpu.make_async_remote_copy(
            src_ref=src, dst_ref=src, send_sem=bs_sem.at[k], recv_sem=br_sem.at[n],
            device_id={"axial": other(*off)}, device_id_type=MESH,
        )
        copy.start()
        bias_sends.append(copy)

    def bias_wait(ref, n):
        pltpu.make_async_copy(ref, ref, br_sem.at[n]).wait()

    for dz in range(1, NZ):
        bias_send(bias_all.at[my_y, my_z, my_c], dz - 1, 0, (dz, 0, 0))

    def exchange(c, src, dst, send_sem, recv_sem):
        for off in OFFSETS:
            to = other(*off)
            pltpu.make_async_remote_copy(
                src_ref=src.at[c * N + to], dst_ref=dst.at[c * N + me], send_sem=send_sem.at[c], recv_sem=recv_sem.at[c],
                device_id={"axial": to}, device_id_type=MESH,
            ).start()
        dst[c * N + me] = src[c * N + me]

    def arrived(c, ref, sem):
        part = ref.at[pl.ds(c * N, N - 1)]
        pltpu.make_async_copy(part, part, sem.at[c]).wait()

    exchange(0, send1, recv1, s1_sem, r1_sem)

    for n in range(4, len(loads)):
        loads[n].wait()
    w_t[0:C] = wq_v[...].astype(jnp.float32).T.astype(jnp.bfloat16)
    w_t[C : 2 * C] = wv_v[...].astype(jnp.float32).T.astype(jnp.bfloat16)
    w_t[2 * C : 3 * C] = wg_v[...].astype(jnp.float32).T.astype(jnp.bfloat16)
    gate_bias_t[...] = jnp.broadcast_to(gb_v[...], (C, C)).T

    bias_wait(bias_all.at[my_y, pl.ds(0, NZ - 1), my_c], 0)
    mine = bias_all.at[my_y, :, my_c]
    bias_send(mine, 7, 1, (0, 1, 0))
    bias_send(mine, 8, 2, (0, 0, 1))
    for c in range(1, CHUNKS):
        exchange(c, send1, recv1, s1_sem, r1_sem)
    bias_wait(mine, 1)
    bias_send(bias_all.at[1 - my_y, :, my_c], 9, 3, (0, 0, 1))
    bias_wait(mine, 2)
    bias_wait(mine, 3)
    for h in range(H):
        part = bias_all[:, :, :, h * ROWS : (h + 1) * ROWS, :]
        bias_f[h] = part.astype(jnp.float32).reshape(RES, RES)

    lane_head = lax.broadcasted_iota(jnp.int32, (RES, C), 1) // DH
    scale = 1.0 / DH**0.5

    def column(x_j):
        key_rows = dot_nn(x_j, wk_v[...])
        turned = dot_nt(w_t[...], x_j)
        queries = (turned[0:C] * scale).astype(jnp.bfloat16)
        values = turned[C : 2 * C].astype(jnp.bfloat16)
        gate_bias = gate_bias_t[...]
        gating = jax.nn.sigmoid(turned[2 * C :] + jnp.concatenate([gate_bias, gate_bias], axis=1))
        outs = []
        for h in range(H):
            key_h = jnp.where(lane_head == h, key_rows, 0.0).astype(jnp.bfloat16)
            scores = dot_nn(key_h, queries) + bias_f[h]
            highest = jnp.max(scores, axis=0, keepdims=True)
            expo = jnp.exp(scores - highest)
            total = jnp.sum(expo, axis=0, keepdims=True)
            summed = dot_nn(values[h * DH : (h + 1) * DH], expo.astype(jnp.bfloat16))
            outs.append(summed / total)
        attended = jnp.concatenate(outs, axis=0)
        gated = (gating * attended).T.astype(jnp.bfloat16)
        return dot_nn(gated, wo_v[...]) + ob_v[...]

    for c in range(CHUNKS):
        arrived(c, recv1, r1_sem)

        def pair(p, carry, c=c):
            rows = pl.ds(pl.multiple_of(p * 2 * ROWS, 2 * ROWS), 2 * ROWS)
            both = recv1[pl.ds(c * N, N), rows, :].astype(jnp.float32).reshape(N, 2, ROWS, C)
            done = [column(both[:, q].reshape(RES, C).astype(jnp.bfloat16)).reshape(N, ROWS, C) for q in range(2)]
            send2[pl.ds(c * N, N), rows, :] = jnp.concatenate(done, axis=1).astype(jnp.bfloat16)
            return carry

        lax.fori_loop(0, COLS // 2, pair, 0)
        exchange(c, send2, out_ref, s2_sem, r2_sem)

    for c in range(CHUNKS):
        arrived(c, out_ref, r2_sem)
    for copy in bias_sends:
        copy.wait_send()
    for c in range(CHUNKS):
        arrived(c, send1, s1_sem)
        arrived(c, send2, s2_sem)


def on_device(x, gain, shift, wq, wk, wv, wb, wg, gb, wo, ob):
    blocks = jax.ShapeDtypeStruct((CHUNKS * N, MSG, C), jnp.bfloat16)
    bf16, f32 = jnp.bfloat16, jnp.float32
    out = pl.pallas_call(
        kernel,
        out_shape=blocks,
        in_specs=[pl.BlockSpec(memory_space=pltpu.HBM)] * 11,
        out_specs=pl.BlockSpec(memory_space=pltpu.VMEM),
        scratch_shapes=[
            pltpu.VMEM((ROWS, RES, C), bf16),
            pltpu.VMEM((1, C), f32),
            pltpu.VMEM((1, C), f32),
            pltpu.VMEM((C, C), bf16),
            pltpu.VMEM((C, C), bf16),
            pltpu.VMEM((C, C), bf16),
            pltpu.VMEM((H, C), bf16),
            pltpu.VMEM((C, C), bf16),
            pltpu.VMEM((1, C), f32),
            pltpu.VMEM((C, C), bf16),
            pltpu.VMEM((1, C), f32),
            pltpu.VMEM(blocks.shape, bf16),
            pltpu.VMEM(blocks.shape, bf16),
            pltpu.VMEM(blocks.shape, bf16),
            pltpu.VMEM((NY, NZ, NCORE, H * ROWS, RES), bf16),
            pltpu.VMEM((H, RES, RES), f32),
            pltpu.VMEM((3 * C, C), bf16),
            pltpu.VMEM((C, C), f32),
            pltpu.SemaphoreType.DMA((11,)),
            pltpu.SemaphoreType.DMA((CHUNKS,)),
            pltpu.SemaphoreType.DMA((CHUNKS,)),
            pltpu.SemaphoreType.DMA((CHUNKS,)),
            pltpu.SemaphoreType.DMA((CHUNKS,)),
            pltpu.SemaphoreType.DMA((10,)),
            pltpu.SemaphoreType.DMA((4,)),
        ],
        compiler_params=pltpu.CompilerParams(
            collective_id=0, has_side_effects=True, vmem_limit_bytes=60 * 2**20
        ),
    )(
        x, gain.reshape(1, C), shift.reshape(1, C), wq, wk, wv, wb.T, wg, gb.reshape(1, C), wo, ob.reshape(1, C)
    )
    return jnp.swapaxes(out.reshape(RES, ROWS, C), 0, 1)


def solution(mesh):
    return jax.shard_map(
        on_device,
        mesh=mesh,
        in_specs=(P(("dp", "axial"), None, None), P(), P(), P(), P(), P(), P(), P(), P(), P(), P()),
        out_specs=P(("dp", "axial"), None, None),
        check_vma=False,
    )
```

```python
import functools

import jax
import jax.numpy as jnp
from jax import lax
from jax.experimental import pallas as pl
from jax.experimental.pallas import tpu as pltpu
from jax.sharding import PartitionSpec as P

MESH = pl.DeviceIdType.MESH
NZ, NY, NCORE = 8, 2, 2
N = NZ * NY * NCORE
ROWS = 8
RES = 256
C = 128
H = 4
DH = 32
CHUNKS = 4
COLS = RES // N // CHUNKS
MSG = COLS * ROWS

OFFSETS = [(dz, dy, dc) for dz in range(NZ) for dy in range(NY) for dc in range(NCORE)][1:]

NT = (((1,), (1,)), ((), ()))


def dot_nt(a, b):
    return lax.dot_general(a, b, NT, preferred_element_type=jnp.float32)


def dot_nn(a, b):
    return jnp.dot(a, b, preferred_element_type=jnp.float32)


def kernel(
    x_hbm, gain_hbm, offset_hbm, wq_hbm, wk_hbm, wv_hbm, wb_hbm, wg_hbm, gb_hbm, wo_hbm, ob_hbm,
    out_ref,
    x_v, gain_v, offset_v, wb_v, w_all, gb_v, wo_v, ob_v,
    send1, recv1, send2, bias_all, bias_f,
    load_sem, s1_sem, r1_sem, s2_sem, r2_sem, bs_sem, bz_sem, by_sem, bc_sem,
):
    me = lax.axis_index("axial")
    my_y, my_z, my_c = me // (NZ * NCORE), (me // NCORE) % NZ, me % NCORE

    def other(dz, dy, dc):
        return ((my_y + dy) % NY) * (NZ * NCORE) + ((my_z + dz) % NZ) * NCORE + (my_c + dc) % NCORE

    loads = []
    for n, (src, dst) in enumerate(
        [
            (x_hbm, x_v), (gain_hbm, gain_v), (offset_hbm, offset_v), (wb_hbm, wb_v),
            (wq_hbm, w_all.at[:, 0:C]), (wk_hbm, w_all.at[:, C : 2 * C]),
            (wv_hbm, w_all.at[:, 2 * C : 3 * C]), (wg_hbm, w_all.at[:, 3 * C : 4 * C]), (gb_hbm, gb_v), (wo_hbm, wo_v), (ob_hbm, ob_v),
        ]
    ):
        copy = pltpu.make_async_copy(src, dst, load_sem.at[n])
        copy.start()
        loads.append(copy)

    barrier = pltpu.get_barrier_semaphore()
    for off in OFFSETS:
        pl.semaphore_signal(barrier, inc=1, device_id={"axial": other(*off)}, device_id_type=MESH)

    for n in range(4):
        loads[n].wait()

    gain = gain_v[...][None]
    shift = offset_v[...][None]
    wb = wb_v[...].astype(jnp.float32)
    wb_rep = jnp.broadcast_to(wb[:, None, :], (H, ROWS, C)).reshape(H * ROWS, C)
    row_of = lax.broadcasted_iota(jnp.int32, (H * ROWS, C), 0) % ROWS
    wb_row = [jnp.where(row_of == r, wb_rep, 0.0).astype(jnp.bfloat16) for r in range(ROWS)]

    STEP = 32
    for block in range(RES // STEP):
        values = x_v[:, pl.ds(block * STEP, STEP), :].astype(jnp.float32)
        average = jnp.mean(values, axis=-1, keepdims=True)
        centred = values - average
        spread = jnp.mean(centred * centred, axis=-1, keepdims=True)
        scaled = centred * lax.rsqrt(spread + 1e-05) * gain + shift
        turned = jnp.swapaxes(scaled, 0, 1).reshape(STEP // 2, 2 * ROWS, C)
        turned = turned.astype(jnp.bfloat16).reshape(STEP * ROWS // MSG, MSG, C)
        first = block * STEP * ROWS // MSG
        send1[pl.ds(first, STEP * ROWS // MSG)] = turned
        x_v[:, pl.ds(block * STEP, STEP), :] = scaled.astype(jnp.bfloat16)

    acc = dot_nt(wb_row[0], x_v[0])
    for r in range(1, ROWS):
        acc = acc + dot_nt(wb_row[r], x_v[r])
    bias_all[me] = acc.astype(jnp.bfloat16)

    pl.semaphore_wait(barrier, N - 1)

    def bias_send(slot, sem, off):
        block = bias_all.at[slot]
        pltpu.make_async_remote_copy(
            src_ref=block, dst_ref=block, send_sem=bs_sem.at[0], recv_sem=sem,
            device_id={"axial": other(*off)}, device_id_type=MESH,
        ).start()

    def bias_wait(sem, count=1):
        blocks = bias_all.at[pl.ds(0, count)]
        pltpu.make_async_copy(blocks, blocks, sem).wait()

    def slot_of(dz, dy, dc=0):
        return other(NZ - dz, dy, dc)

    for dz in (4, 3, 5, 2, 6, 1, 7):
        bias_send(me, bz_sem.at[dz], (dz, 0, 0))
    bias_send(me, by_sem.at[0], (0, 1, 0))
    bias_send(me, bc_sem.at[0], (0, 0, 1))

    def exchange(c, src, dst, send_sem, recv_sem):
        for off in OFFSETS:
            to = other(*off)
            pltpu.make_async_remote_copy(
                src_ref=src.at[c * N + to], dst_ref=dst.at[c * N + me], send_sem=send_sem.at[c], recv_sem=recv_sem.at[c],
                device_id={"axial": to}, device_id_type=MESH,
            ).start()
        dst[c * N + me] = src[c * N + me]

    def arrived(c, ref, sem):
        part = ref.at[pl.ds(c * N, N - 1)]
        pltpu.make_async_copy(part, part, sem.at[c]).wait()

    for c in range(CHUNKS):
        exchange(c, send1, recv1, s1_sem, r1_sem)

    for step in ("z1", "z7", "y0", "z2", "z6", "y1", "y7", "z3", "z5", "y2", "y6", "z4", "y3", "y5"):
        dz = int(step[1])
        if step[0] == "z":
            bias_wait(bz_sem.at[dz])
            bias_send(slot_of(dz, 0), by_sem.at[dz], (0, 1, 0))
            bias_send(slot_of(dz, 0), bc_sem.at[0], (0, 0, 1))
        else:
            bias_wait(by_sem.at[dz])
            bias_send(slot_of(dz, 1), bc_sem.at[1], (0, 0, 1))

    def bias_half(y):
        lanes = pl.ds(pl.multiple_of(y * (RES // NY), RES // NY), RES // NY)
        slots = pl.ds(y * NZ * NCORE, NZ * NCORE)
        for h in range(H):
            part = bias_all[slots, h * ROWS : (h + 1) * ROWS, :]
            bias_f[h, :, lanes] = part.astype(jnp.float32).reshape(RES // NY, RES).T

    bias_wait(bc_sem.at[0], NZ)
    bias_half(my_y)
    bias_wait(by_sem.at[4])
    bias_send(slot_of(4, 1), bc_sem.at[1], (0, 0, 1))
    for n in range(4, len(loads)):
        loads[n].wait()
    bias_wait(bc_sem.at[1], NZ)
    bias_half(1 - my_y)

    lane_head = lax.broadcasted_iota(jnp.int32, (RES, C), 1) // DH
    scale = 1.0 / DH**0.5

    def attend(projected):
        queries = projected[:, 0:C] * scale
        keys = projected[:, C : 2 * C].astype(jnp.bfloat16)
        values = projected[:, 2 * C : 3 * C].astype(jnp.bfloat16)
        gating = jax.nn.sigmoid(projected[:, 3 * C :] + gb_v[...])
        for h in range(H):
            own = lane_head == h
            query_h = jnp.where(own, queries, 0.0).astype(jnp.bfloat16)
            scores = dot_nt(query_h, keys) + bias_f[h]
            expo = jnp.exp(scores - jnp.max(scores, axis=1, keepdims=True))
            total = jnp.broadcast_to(jnp.sum(expo, axis=1, keepdims=True), (RES, C))
            part = dot_nn(expo.astype(jnp.bfloat16), values)
            summed = part if h == 0 else jnp.where(own, part, summed)
            totals = total if h == 0 else jnp.where(own, total, totals)
        return (gating * (summed / totals)).astype(jnp.bfloat16)

    for c in range(CHUNKS):
        arrived(c, recv1, r1_sem)
        block = recv1[pl.ds(c * N, N)].astype(jnp.float32).reshape(N, COLS, ROWS, C)
        columns = jnp.concatenate([block[:, q].reshape(RES, C) for q in range(COLS)], axis=0).astype(jnp.bfloat16)
        projected = dot_nn(columns, w_all[...])
        gated = jnp.concatenate([attend(projected[q * RES : (q + 1) * RES]) for q in range(COLS)], axis=0)
        update = dot_nn(gated, wo_v[...]) + ob_v[...]
        parts = [update[q * RES : (q + 1) * RES].reshape(N, ROWS, C) for q in range(COLS)]
        send2[pl.ds(c * N, N)] = jnp.concatenate(parts, axis=1).astype(jnp.bfloat16)
        exchange(c, send2, out_ref, s2_sem, r2_sem)

    for c in range(CHUNKS):
        arrived(c, out_ref, r2_sem)
    bias_wait(bs_sem.at[0], NZ - 1 + 3 * NZ)
    for c in range(CHUNKS):
        arrived(c, send1, s1_sem)
        arrived(c, send2, s2_sem)


def on_device(x, gain, shift, wq, wk, wv, wb, wg, gb, wo, ob):
    blocks = jax.ShapeDtypeStruct((CHUNKS * N, MSG, C), jnp.bfloat16)
    bf16, f32 = jnp.bfloat16, jnp.float32
    out = pl.pallas_call(
        kernel,
        out_shape=blocks,
        in_specs=[pl.BlockSpec(memory_space=pltpu.HBM)] * 11,
        out_specs=pl.BlockSpec(memory_space=pltpu.VMEM),
        scratch_shapes=[
            pltpu.VMEM((ROWS, RES, C), bf16),
            pltpu.VMEM((1, C), f32),
            pltpu.VMEM((1, C), f32),
            pltpu.VMEM((H, C), bf16),
            pltpu.VMEM((C, 4 * C), bf16),
            pltpu.VMEM((1, C), f32),
            pltpu.VMEM((C, C), bf16),
            pltpu.VMEM((1, C), f32),
            pltpu.VMEM(blocks.shape, bf16),
            pltpu.VMEM(blocks.shape, bf16),
            pltpu.VMEM(blocks.shape, bf16),
            pltpu.VMEM((N, H * ROWS, RES), bf16),
            pltpu.VMEM((H, RES, RES), f32),
            pltpu.SemaphoreType.DMA((11,)),
            pltpu.SemaphoreType.DMA((CHUNKS,)),
            pltpu.SemaphoreType.DMA((CHUNKS,)),
            pltpu.SemaphoreType.DMA((CHUNKS,)),
            pltpu.SemaphoreType.DMA((CHUNKS,)),
            pltpu.SemaphoreType.DMA((1,)),
            pltpu.SemaphoreType.DMA((NZ,)),
            pltpu.SemaphoreType.DMA((NZ,)),
            pltpu.SemaphoreType.DMA((NCORE,)),
        ],
        compiler_params=pltpu.CompilerParams(
            collective_id=0, has_side_effects=True, vmem_limit_bytes=40 * 2**20
        ),
    )(
        *[pltpu.with_memory_space_constraint(a, pltpu.HBM) for a in (x, gain.reshape(1, C), shift.reshape(1, C), wq, wk, wv, wb.T, wg, gb.reshape(1, C), wo, ob.reshape(1, C))]
    )
    return jnp.swapaxes(out.reshape(RES, ROWS, C), 0, 1)


def solution(mesh):
    return jax.shard_map(
        on_device,
        mesh=mesh,
        in_specs=(P(("dp", "axial"), None, None), P(), P(), P(), P(), P(), P(), P(), P(), P(), P()),
        out_specs=P(("dp", "axial"), None, None),
        check_vma=False,
    )
```

```python
import functools

import jax
import jax.numpy as jnp
from jax import lax
from jax.experimental import pallas as pl
from jax.experimental.pallas import tpu as pltpu
from jax.sharding import PartitionSpec as P

MESH = pl.DeviceIdType.MESH
NZ, NY, NCORE = 8, 2, 2
N = NZ * NY * NCORE
ROWS = 8
RES = 256
C = 128
H = 4
DH = 32
CHUNKS = 4
COLS = RES // N // CHUNKS
MSG = COLS * ROWS

OFFSETS = [(dz, dy, dc) for dz in (4, 3, 5, 2, 6, 1, 7, 0) for dy in (1, 0) for dc in range(NCORE)][:-2] + [(0, 0, 1)]

NT = (((1,), (1,)), ((), ()))


def dot_nt(a, b):
    return lax.dot_general(a, b, NT, preferred_element_type=jnp.float32)


def dot_nn(a, b):
    return jnp.dot(a, b, preferred_element_type=jnp.float32)


def kernel(
    x_hbm, gain_hbm, offset_hbm, wq_hbm, wk_hbm, wv_hbm, wb_hbm, wg_hbm, gb_hbm, wo_hbm, ob_hbm,
    out_ref,
    x_v, gain_v, offset_v, wb_v, w_all, gb_v, wo_v, ob_v,
    send1, recv1, send2, bias_all, bias_f,
    load_sem, s1_sem, r1_sem, s2_sem, r2_sem, bs_sem, bz_sem, by_sem, bc_sem,
):
    me = lax.axis_index("axial")
    my_y, my_z, my_c = me // (NZ * NCORE), (me // NCORE) % NZ, me % NCORE

    def other(dz, dy, dc):
        return ((my_y + dy) % NY) * (NZ * NCORE) + ((my_z + dz) % NZ) * NCORE + (my_c + dc) % NCORE

    loads = []
    for n, (src, dst) in enumerate(
        [
            (x_hbm, x_v), (gain_hbm, gain_v), (offset_hbm, offset_v), (wb_hbm, wb_v),
            (wq_hbm, w_all.at[:, 0:C]), (wk_hbm, w_all.at[:, C : 2 * C]),
            (wv_hbm, w_all.at[:, 2 * C : 3 * C]), (wg_hbm, w_all.at[:, 3 * C : 4 * C]), (gb_hbm, gb_v), (wo_hbm, wo_v), (ob_hbm, ob_v),
        ]
    ):
        copy = pltpu.make_async_copy(src, dst, load_sem.at[n])
        copy.start()
        loads.append(copy)

    barrier = pltpu.get_barrier_semaphore()
    for off in OFFSETS:
        pl.semaphore_signal(barrier, inc=1, device_id={"axial": other(*off)}, device_id_type=MESH)

    for n in range(4):
        loads[n].wait()

    gain = gain_v[...][None]
    shift = offset_v[...][None]
    wb = wb_v[...].astype(jnp.float32)
    wb_rep = jnp.broadcast_to(wb[:, None, :], (H, ROWS, C)).reshape(H * ROWS, C)
    row_of = lax.broadcasted_iota(jnp.int32, (H * ROWS, C), 0) % ROWS
    wb_row = [jnp.where(row_of == r, wb_rep, 0.0).astype(jnp.bfloat16) for r in range(ROWS)]

    STEP = 32
    for block in range(RES // STEP):
        values = x_v[:, pl.ds(block * STEP, STEP), :].astype(jnp.float32)
        average = jnp.mean(values, axis=-1, keepdims=True)
        centred = values - average
        spread = jnp.mean(centred * centred, axis=-1, keepdims=True)
        scaled = centred * lax.rsqrt(spread + 1e-05) * gain + shift
        turned = jnp.swapaxes(scaled, 0, 1).reshape(STEP // 2, 2 * ROWS, C)
        turned = turned.astype(jnp.bfloat16).reshape(STEP * ROWS // MSG, MSG, C)
        first = block * STEP * ROWS // MSG
        send1[pl.ds(first, STEP * ROWS // MSG)] = turned
        x_v[:, pl.ds(block * STEP, STEP), :] = scaled.astype(jnp.bfloat16)

    acc = dot_nt(wb_row[0], x_v[0])
    for r in range(1, ROWS):
        acc = acc + dot_nt(wb_row[r], x_v[r])
    bias_all[me] = acc.astype(jnp.bfloat16)

    pl.semaphore_wait(barrier, N - 1)

    def bias_send(slot, sem, off):
        block = bias_all.at[slot]
        pltpu.make_async_remote_copy(
            src_ref=block, dst_ref=block, send_sem=bs_sem.at[0], recv_sem=sem,
            device_id={"axial": other(*off)}, device_id_type=MESH,
        ).start()

    def bias_wait(sem, count=1):
        blocks = bias_all.at[pl.ds(0, count)]
        pltpu.make_async_copy(blocks, blocks, sem).wait()

    def slot_of(dz, dy, dc=0):
        return other(NZ - dz, dy, dc)

    for dz in (4, 3, 5, 2, 6, 1, 7):
        bias_send(me, bz_sem.at[dz], (dz, 0, 0))
    bias_send(me, by_sem.at[0], (0, 1, 0))
    bias_send(me, bc_sem.at[0], (0, 0, 1))

    def exchange(c, src, dst, send_sem, recv_sem, offsets=OFFSETS):
        for off in offsets:
            to = other(*off)
            pltpu.make_async_remote_copy(
                src_ref=src.at[c * N + to], dst_ref=dst.at[c * N + me], send_sem=send_sem.at[c], recv_sem=recv_sem.at[c],
                device_id={"axial": to}, device_id_type=MESH,
            ).start()

    def keep(c, src, dst):
        dst[c * N + me] = src[c * N + me]

    def arrived(c, ref, sem):
        part = ref.at[pl.ds(c * N, N - 1)]
        pltpu.make_async_copy(part, part, sem.at[c]).wait()

    for c in range(2):
        exchange(c, send1, recv1, s1_sem, r1_sem, [off for off in OFFSETS if off[1] == 0])
    for dz in (1, 7, 2, 6, 3, 5, 4):
        bias_wait(bz_sem.at[dz])
        bias_send(slot_of(dz, 0), by_sem.at[dz], (0, 1, 0))
        bias_send(slot_of(dz, 0), bc_sem.at[0], (0, 0, 1))
    for c in range(2):
        exchange(c, send1, recv1, s1_sem, r1_sem, [off for off in OFFSETS if off[1] == 1])
    for c in range(2, CHUNKS):
        exchange(c, send1, recv1, s1_sem, r1_sem)
    for c in range(CHUNKS):
        keep(c, send1, recv1)
    for dz in (0, 1, 7, 2, 6):
        bias_wait(by_sem.at[dz])
        bias_send(slot_of(dz, 1), bc_sem.at[1], (0, 0, 1))

    def bias_half(y):
        lanes = pl.ds(pl.multiple_of(y * (RES // NY), RES // NY), RES // NY)
        slots = pl.ds(y * NZ * NCORE, NZ * NCORE)
        for h in range(H):
            part = bias_all[slots, h * ROWS : (h + 1) * ROWS, :]
            bias_f[h, :, lanes] = part.astype(jnp.float32).reshape(RES // NY, RES).T

    bias_wait(bc_sem.at[0], NZ)
    bias_half(my_y)
    for dz in (3, 5, 4):
        bias_wait(by_sem.at[dz])
        bias_send(slot_of(dz, 1), bc_sem.at[1], (0, 0, 1))
    for n in range(4, len(loads)):
        loads[n].wait()
    bias_wait(bc_sem.at[1], NZ)
    bias_half(1 - my_y)

    lane_head = lax.broadcasted_iota(jnp.int32, (RES, C), 1) // DH
    scale = 1.0 / DH**0.5

    def attend(projected):
        queries = projected[:, 0:C] * scale
        keys = projected[:, C : 2 * C].astype(jnp.bfloat16)
        values = projected[:, 2 * C : 3 * C].astype(jnp.bfloat16)
        gating = jax.nn.sigmoid(projected[:, 3 * C :] + gb_v[...])
        for h in range(H):
            own = lane_head == h
            query_h = jnp.where(own, queries, 0.0).astype(jnp.bfloat16)
            scores = dot_nt(query_h, keys) + bias_f[h]
            expo = jnp.exp(scores - jnp.max(scores, axis=1, keepdims=True))
            total = jnp.broadcast_to(jnp.sum(expo, axis=1, keepdims=True), (RES, C))
            part = dot_nn(expo.astype(jnp.bfloat16), values)
            summed = part if h == 0 else jnp.where(own, part, summed)
            totals = total if h == 0 else jnp.where(own, total, totals)
        return (gating * (summed / totals)).astype(jnp.bfloat16)

    for c in range(CHUNKS):
        arrived(c, recv1, r1_sem)
        block = recv1[pl.ds(c * N, N)].astype(jnp.float32).reshape(N, COLS, ROWS, C)
        columns = jnp.concatenate([block[:, q].reshape(RES, C) for q in range(COLS)], axis=0).astype(jnp.bfloat16)
        projected = dot_nn(columns, w_all[...])
        gated = jnp.concatenate([attend(projected[q * RES : (q + 1) * RES]) for q in range(COLS)], axis=0)
        update = dot_nn(gated, wo_v[...]) + ob_v[...]
        parts = [update[q * RES : (q + 1) * RES].reshape(N, ROWS, C) for q in range(COLS)]
        send2[pl.ds(c * N, N)] = jnp.concatenate(parts, axis=1).astype(jnp.bfloat16)
        for z in (0, 1, 2, 3, 7, 4, 6, 5):
            for y in range(NY):
                for core in range(NCORE):
                    to = y * NZ * NCORE + z * NCORE + core

                    @pl.when(to != me)
                    def _(to=to, c=c):
                        pltpu.make_async_remote_copy(
                            src_ref=send2.at[c * N + to], dst_ref=out_ref.at[c * N + me], send_sem=s2_sem.at[c],
                            recv_sem=r2_sem.at[c], device_id={"axial": to}, device_id_type=MESH,
                        ).start()

        keep(c, send2, out_ref)

    for c in range(CHUNKS):
        arrived(c, out_ref, r2_sem)
    bias_wait(bs_sem.at[0], NZ - 1 + 3 * NZ)
    for c in range(CHUNKS):
        arrived(c, send1, s1_sem)
        arrived(c, send2, s2_sem)


def on_device(x, gain, shift, wq, wk, wv, wb, wg, gb, wo, ob):
    blocks = jax.ShapeDtypeStruct((CHUNKS * N, MSG, C), jnp.bfloat16)
    bf16, f32 = jnp.bfloat16, jnp.float32
    out = pl.pallas_call(
        kernel,
        out_shape=blocks,
        in_specs=[pl.BlockSpec(memory_space=pltpu.HBM)] * 11,
        out_specs=pl.BlockSpec(memory_space=pltpu.VMEM),
        scratch_shapes=[
            pltpu.VMEM((ROWS, RES, C), bf16),
            pltpu.VMEM((1, C), f32),
            pltpu.VMEM((1, C), f32),
            pltpu.VMEM((H, C), bf16),
            pltpu.VMEM((C, 4 * C), bf16),
            pltpu.VMEM((1, C), f32),
            pltpu.VMEM((C, C), bf16),
            pltpu.VMEM((1, C), f32),
            pltpu.VMEM(blocks.shape, bf16),
            pltpu.VMEM(blocks.shape, bf16),
            pltpu.VMEM(blocks.shape, bf16),
            pltpu.VMEM((N, H * ROWS, RES), bf16),
            pltpu.VMEM((H, RES, RES), f32),
            pltpu.SemaphoreType.DMA((11,)),
            pltpu.SemaphoreType.DMA((CHUNKS,)),
            pltpu.SemaphoreType.DMA((CHUNKS,)),
            pltpu.SemaphoreType.DMA((CHUNKS,)),
            pltpu.SemaphoreType.DMA((CHUNKS,)),
            pltpu.SemaphoreType.DMA((1,)),
            pltpu.SemaphoreType.DMA((NZ,)),
            pltpu.SemaphoreType.DMA((NZ,)),
            pltpu.SemaphoreType.DMA((NCORE,)),
        ],
        compiler_params=pltpu.CompilerParams(
            collective_id=0, has_side_effects=True, vmem_limit_bytes=40 * 2**20
        ),
    )(
        *[pltpu.with_memory_space_constraint(a, pltpu.HBM) for a in (x, gain.reshape(1, C), shift.reshape(1, C), wq, wk, wv, wb.T, wg, gb.reshape(1, C), wo, ob.reshape(1, C))]
    )
    return jnp.swapaxes(out.reshape(RES, ROWS, C), 0, 1)


def solution(mesh):
    return jax.shard_map(
        on_device,
        mesh=mesh,
        in_specs=(P(("dp", "axial"), None, None), P(), P(), P(), P(), P(), P(), P(), P(), P(), P()),
        out_specs=P(("dp", "axial"), None, None),
        check_vma=False,
    )
```

```python
import functools

import jax
import jax.numpy as jnp
from jax import lax
from jax.experimental import pallas as pl
from jax.experimental.pallas import tpu as pltpu
from jax.sharding import PartitionSpec as P

MESH = pl.DeviceIdType.MESH
NZ, NY, NCORE = 8, 2, 2
N = NZ * NY * NCORE
ROWS = 8
RES = 256
C = 128
H = 4
DH = 32
CHUNKS = 4
COLS = RES // N // CHUNKS
MSG = COLS * ROWS

OFFSETS = [(dz, dy, dc) for dz in (4, 3, 5, 2, 6, 1, 7, 0) for dy in (1, 0) for dc in range(NCORE)][:-2] + [(0, 0, 1)]

NT = (((1,), (1,)), ((), ()))


def dot_nt(a, b):
    return lax.dot_general(a, b, NT, preferred_element_type=jnp.float32)


def dot_nn(a, b):
    return jnp.dot(a, b, preferred_element_type=jnp.float32)


def kernel(
    x_hbm, gain_hbm, offset_hbm, wq_hbm, wk_hbm, wv_hbm, wb_hbm, wg_hbm, gb_hbm, wo_hbm, ob_hbm,
    out_ref,
    x_v, gain_v, offset_v, wb_v, w_all, gb_v, wo_v, ob_v,
    send1, recv1, send2, got, bias_all, bias_f,
    load_sem, s1_sem, r1_sem, s2_sem, r2_sem, bs_sem, bz_sem, by_sem, bc_sem,
):
    me = lax.axis_index("axial")
    my_y, my_z, my_c = me // (NZ * NCORE), (me // NCORE) % NZ, me % NCORE

    def other(dz, dy, dc):
        return ((my_y + dy) % NY) * (NZ * NCORE) + ((my_z + dz) % NZ) * NCORE + (my_c + dc) % NCORE

    loads = []
    for n, (src, dst) in enumerate(
        [
            (x_hbm, x_v), (gain_hbm, gain_v), (offset_hbm, offset_v), (wb_hbm, wb_v),
            (wq_hbm, w_all.at[:, 0:C]), (wk_hbm, w_all.at[:, C : 2 * C]),
            (wv_hbm, w_all.at[:, 2 * C : 3 * C]), (wg_hbm, w_all.at[:, 3 * C : 4 * C]), (gb_hbm, gb_v), (wo_hbm, wo_v), (ob_hbm, ob_v),
        ]
    ):
        copy = pltpu.make_async_copy(src, dst, load_sem.at[n])
        copy.start()
        loads.append(copy)

    barrier = pltpu.get_barrier_semaphore()
    for off in OFFSETS:
        pl.semaphore_signal(barrier, inc=1, device_id={"axial": other(*off)}, device_id_type=MESH)

    for n in range(4):
        loads[n].wait()

    gain = gain_v[...][None]
    shift = offset_v[...][None]
    wb = wb_v[...].astype(jnp.float32)
    wb_rep = jnp.broadcast_to(wb[:, None, :], (H, ROWS, C)).reshape(H * ROWS, C)
    row_of = lax.broadcasted_iota(jnp.int32, (H * ROWS, C), 0) % ROWS
    wb_row = [jnp.where(row_of == r, wb_rep, 0.0).astype(jnp.bfloat16) for r in range(ROWS)]

    STEP = 32
    for block in range(RES // STEP):
        values = x_v[:, pl.ds(block * STEP, STEP), :].astype(jnp.float32)
        average = jnp.mean(values, axis=-1, keepdims=True)
        centred = values - average
        spread = jnp.mean(centred * centred, axis=-1, keepdims=True)
        scaled = centred * lax.rsqrt(spread + 1e-05) * gain + shift
        turned = jnp.swapaxes(scaled, 0, 1).reshape(STEP // 2, 2 * ROWS, C)
        turned = turned.astype(jnp.bfloat16).reshape(STEP * ROWS // MSG, MSG, C)
        first = block * STEP * ROWS // MSG
        send1[pl.ds(first, STEP * ROWS // MSG)] = turned
        x_v[:, pl.ds(block * STEP, STEP), :] = scaled.astype(jnp.bfloat16)

    acc = dot_nt(wb_row[0], x_v[0])
    for r in range(1, ROWS):
        acc = acc + dot_nt(wb_row[r], x_v[r])
    bias_all[me] = acc.astype(jnp.bfloat16)

    pl.semaphore_wait(barrier, N - 1)

    def bias_send(slot, sem, off):
        block = bias_all.at[slot]
        pltpu.make_async_remote_copy(
            src_ref=block, dst_ref=block, send_sem=bs_sem.at[0], recv_sem=sem,
            device_id={"axial": other(*off)}, device_id_type=MESH,
        ).start()

    def bias_wait(sem, count=1):
        blocks = bias_all.at[pl.ds(0, count)]
        pltpu.make_async_copy(blocks, blocks, sem).wait()

    def slot_of(dz, dy, dc=0):
        return other(NZ - dz, dy, dc)

    for dz in (4, 3, 5, 2, 6, 1, 7):
        bias_send(me, bz_sem.at[dz], (dz, 0, 0))
    bias_send(me, by_sem.at[0], (0, 1, 0))
    bias_send(me, bc_sem.at[0], (0, 0, 1))

    def exchange(c, src, dst, send_sem, recv_sem, offsets=OFFSETS):
        for off in offsets:
            to = other(*off)
            pltpu.make_async_remote_copy(
                src_ref=src.at[c * N + to], dst_ref=dst.at[c * N + me], send_sem=send_sem.at[c], recv_sem=recv_sem.at[c],
                device_id={"axial": to}, device_id_type=MESH,
            ).start()

    def keep(c, src, dst):
        dst[c * N + me] = src[c * N + me]

    def arrived(c, ref, sem):
        part = ref.at[pl.ds(c * N, N - 1)]
        pltpu.make_async_copy(part, part, sem.at[c]).wait()

    for c in range(1):
        exchange(c, send1, recv1, s1_sem, r1_sem, [off for off in OFFSETS if off[1] == 0])
    for dz in (1, 7, 2, 6, 3, 5, 4):
        bias_wait(bz_sem.at[dz])
        bias_send(slot_of(dz, 0), by_sem.at[dz], (0, 1, 0))
        bias_send(slot_of(dz, 0), bc_sem.at[0], (0, 0, 1))
    for c in range(1):
        exchange(c, send1, recv1, s1_sem, r1_sem, [off for off in OFFSETS if off[1] == 1])
    for c in range(1, CHUNKS):
        exchange(c, send1, recv1, s1_sem, r1_sem)
    for c in range(CHUNKS):
        keep(c, send1, recv1)
    for dz in (0, 1, 7, 2, 6):
        bias_wait(by_sem.at[dz])
        bias_send(slot_of(dz, 1), bc_sem.at[1], (0, 0, 1))

    def bias_half(y):
        lanes = pl.ds(pl.multiple_of(y * (RES // NY), RES // NY), RES // NY)
        slots = pl.ds(y * NZ * NCORE, NZ * NCORE)
        for h in range(H):
            part = bias_all[slots, h * ROWS : (h + 1) * ROWS, :]
            bias_f[h, :, lanes] = part.astype(jnp.float32).reshape(RES // NY, RES).T

    bias_wait(bc_sem.at[0], NZ)
    bias_half(my_y)
    for dz in (3, 5, 4):
        bias_wait(by_sem.at[dz])
        bias_send(slot_of(dz, 1), bc_sem.at[1], (0, 0, 1))
    for n in range(4, len(loads)):
        loads[n].wait()

    lane_head = lax.broadcasted_iota(jnp.int32, (RES, C), 1) // DH
    scale = 1.0 / DH**0.5

    def attend(projected):
        queries = projected[:, 0:C] * scale
        keys = projected[:, C : 2 * C].astype(jnp.bfloat16)
        values = projected[:, 2 * C : 3 * C].astype(jnp.bfloat16)
        gating = jax.nn.sigmoid(projected[:, 3 * C :] + gb_v[...])
        for h in range(H):
            own = lane_head == h
            query_h = jnp.where(own, queries, 0.0).astype(jnp.bfloat16)
            scores = dot_nt(query_h, keys) + bias_f[h]
            expo = jnp.exp(scores - jnp.max(scores, axis=1, keepdims=True))
            total = jnp.broadcast_to(jnp.sum(expo, axis=1, keepdims=True), (RES, C))
            part = dot_nn(expo.astype(jnp.bfloat16), values)
            summed = part if h == 0 else jnp.where(own, part, summed)
            totals = total if h == 0 else jnp.where(own, total, totals)
        return (gating * (summed / totals)).astype(jnp.bfloat16)

    for c in range(CHUNKS):
        arrived(c, recv1, r1_sem)
        block = recv1[pl.ds(c * N, N)].astype(jnp.float32).reshape(N, COLS, ROWS, C)
        columns = jnp.concatenate([block[:, q].reshape(RES, C) for q in range(COLS)], axis=0).astype(jnp.bfloat16)
        projected = dot_nn(columns, w_all[...])
        if c == 0:
            bias_wait(bc_sem.at[1], NZ)
            bias_half(1 - my_y)
        gated = jnp.concatenate([attend(projected[q * RES : (q + 1) * RES]) for q in range(COLS)], axis=0)
        update = dot_nn(gated, wo_v[...]) + ob_v[...]
        parts = [update[q * RES : (q + 1) * RES].reshape(N, ROWS, C) for q in range(COLS)]
        send2[pl.ds(c * N, N)] = jnp.concatenate(parts, axis=1).astype(jnp.bfloat16)
        for z in (0, 1, 2, 3, 7, 4, 6, 5):
            for y in range(NY):
                for core in range(NCORE):
                    to = y * NZ * NCORE + z * NCORE + core

                    @pl.when(to != me)
                    def _(to=to, c=c):
                        pltpu.make_async_remote_copy(
                            src_ref=send2.at[c * N + to], dst_ref=got.at[c * N + me], send_sem=s2_sem.at[c],
                            recv_sem=r2_sem.at[c], device_id={"axial": to}, device_id_type=MESH,
                        ).start()

        keep(c, send2, got)

    for c in range(CHUNKS):
        arrived(c, got, r2_sem)
        block = got[pl.ds(c * N, N)].astype(jnp.float32).reshape(N * COLS, ROWS, C)
        out_ref[:, pl.ds(c * N * COLS, N * COLS), :] = jnp.swapaxes(block, 0, 1).astype(jnp.bfloat16)
    bias_wait(bs_sem.at[0], NZ - 1 + 3 * NZ)
    for c in range(CHUNKS):
        arrived(c, send1, s1_sem)
        arrived(c, send2, s2_sem)


def on_device(x, gain, shift, wq, wk, wv, wb, wg, gb, wo, ob):
    blocks = jax.ShapeDtypeStruct((CHUNKS * N, MSG, C), jnp.bfloat16)
    bf16, f32 = jnp.bfloat16, jnp.float32
    out = pl.pallas_call(
        kernel,
        out_shape=jax.ShapeDtypeStruct((ROWS, RES, C), bf16),
        in_specs=[pl.BlockSpec(memory_space=pltpu.HBM)] * 11,
        out_specs=pl.BlockSpec(memory_space=pltpu.VMEM),
        scratch_shapes=[
            pltpu.VMEM((ROWS, RES, C), bf16),
            pltpu.VMEM((1, C), f32),
            pltpu.VMEM((1, C), f32),
            pltpu.VMEM((H, C), bf16),
            pltpu.VMEM((C, 4 * C), bf16),
            pltpu.VMEM((1, C), f32),
            pltpu.VMEM((C, C), bf16),
            pltpu.VMEM((1, C), f32),
            pltpu.VMEM(blocks.shape, bf16),
            pltpu.VMEM(blocks.shape, bf16),
            pltpu.VMEM(blocks.shape, bf16),
            pltpu.VMEM(blocks.shape, bf16),
            pltpu.VMEM((N, H * ROWS, RES), bf16),
            pltpu.VMEM((H, RES, RES), f32),
            pltpu.SemaphoreType.DMA((11,)),
            pltpu.SemaphoreType.DMA((CHUNKS,)),
            pltpu.SemaphoreType.DMA((CHUNKS,)),
            pltpu.SemaphoreType.DMA((CHUNKS,)),
            pltpu.SemaphoreType.DMA((CHUNKS,)),
            pltpu.SemaphoreType.DMA((1,)),
            pltpu.SemaphoreType.DMA((NZ,)),
            pltpu.SemaphoreType.DMA((NZ,)),
            pltpu.SemaphoreType.DMA((NCORE,)),
        ],
        compiler_params=pltpu.CompilerParams(
            collective_id=0, has_side_effects=True, vmem_limit_bytes=40 * 2**20
        ),
    )(
        *[pltpu.with_memory_space_constraint(a, pltpu.HBM) for a in (x, gain.reshape(1, C), shift.reshape(1, C), wq, wk, wv, wb.T, wg, gb.reshape(1, C), wo, ob.reshape(1, C))]
    )
    return out


def solution(mesh):
    return jax.shard_map(
        on_device,
        mesh=mesh,
        in_specs=(P(("dp", "axial"), None, None), P(), P(), P(), P(), P(), P(), P(), P(), P(), P()),
        out_specs=P(("dp", "axial"), None, None),
        check_vma=False,
    )
```
